32 devices in a mesh: gx: 4 (over y, x), gy: 8 (over z, core).
Axes of the slice: x: 2, y: 2, z: 4, core: 2. Of those that a mesh axis runs over, the one named last changes fastest.
Arguments:
- e_field: float32 [3, 32, 256, 512], P(None, 'gx', 'gy'), may hold values from -6 to 6
- h_field: float32 [3, 32, 256, 512], P(None, 'gx', 'gy'), may hold values from -6 to 6
- polar: float32 [3, 32, 256, 512], P(None, 'gx', 'gy'), may hold values from -6 to 6
- polar_prev: float32 [3, 32, 256, 512], P(None, 'gx', 'gy'), may hold values from -6 to 6
- material: int32 [32, 256, 512], P('gx', 'gy'), may hold values from 0 to 3
- eps_table: float32 [4], replicated, may hold values from 1 to 6
- delta_table: float32 [4], replicated, may hold values from 0.5 to 4
- omega_table: float32 [4], replicated, may hold values from 0.2 to 1.2
- damping_table: float32 [4], replicated, may hold values from 0.02 to 0.6
- surface_flags: int32 [4, 8], P('gx', 'gy'), may hold values 0 or 1
Outputs:
- e_out: float32 [3, 32, 256, 512], P(None, 'gx', 'gy')
- h_out: float32 [3, 32, 256, 512], P(None, 'gx', 'gy')
- polar_out: float32 [3, 32, 256, 512], P(None, 'gx', 'gy')
- far_field: float32 [2, 2, 4, 16384], replicated
The draws below stay inside these ranges and needn't reach their ends.
All inputs are finite; a program needn't handle non-finite values. No bound on the sum of `surface_flags` on one device may be relied on, other than what follows from the above.
Results may differ from the reference program's by a relative error of at most 0.0003.
Values sent between devices are 32-bit elements; how exact they have to be, the bound alone decides.
A program may use at most 256 MiB of HBM per device.

```python
import math
import jax
import jax.numpy as jnp
from jax import lax

CX = 8
CY = 32
NZ = 512
NMAT = 4
NTH = 64
NPH = 256
NDIR = 16384
ZS = 384
NX = 32
NY = 256
STRETCHES_X = 4
STRETCHES_Y = 8


def place_ends(drawn, stream_key, low, largest):
    index_at = [jax.random.randint(jax.random.fold_in(stream_key, axis), (), 0, length) for axis, length in enumerate(drawn.shape)]
    main_axis = drawn.shape.index(max(drawn.shape))
    beside = index_at[:main_axis] + [(index_at[main_axis] + 1) % drawn.shape[main_axis]] + index_at[main_axis + 1:]
    return drawn.at[tuple(index_at)].set(low).at[tuple(beside)].set(largest)


def level_of(own_key, shape, shards, low, largest):
    loudness, own = 1.0, jax.random.fold_in(own_key, 6)
    for dim, blocks in shards:
        draws = jnp.exp(jax.random.uniform(jax.random.fold_in(own, dim), (blocks,), jnp.float32, low / len(shards), largest / len(shards)))
        loudness = loudness * jnp.repeat(draws, shape[dim] // blocks).reshape([-1 if axis == dim else 1 for axis in range(len(shape))])
    return loudness


def centred(rng, shape, width, bound, pieces=(), kind=jnp.bfloat16):
    gain = level_of(rng, shape, pieces, -0.22, 0.18) if pieces else 1.0
    drawn = jax.random.normal(rng, shape, jnp.float32) * width * gain
    return jnp.minimum(jnp.maximum(drawn, -bound), bound).astype(kind)


def setup_inputs(seed: int = 0) -> dict:
    splits = jax.random.split(jax.random.key(seed), 11)
    e_field = centred(splits[0], (3, NX, NY, NZ), 1.0, 6.0, ((1, 4), (2, 8)), jnp.float32)
    h_field = centred(splits[1], (3, NX, NY, NZ), 1.0, 6.0, ((1, 4), (2, 8)), jnp.float32)
    polar = centred(splits[2], (3, NX, NY, NZ), 1.0, 6.0, ((1, 4), (2, 8)), jnp.float32)
    polar_prev = centred(splits[3], (3, NX, NY, NZ), 1.0, 6.0, ((1, 4), (2, 8)), jnp.float32)
    material = place_ends(jax.random.randint(splits[4], (NX, NY, NZ), 0, NMAT), jax.random.fold_in(splits[4], 1), 0, NMAT - 1).astype(jnp.int32)
    eps_table = jnp.clip(jnp.exp(jax.random.uniform(splits[5], (NMAT,), jnp.float32, math.log(1.0), math.log(6.0))), 1.0, 6.0)
    delta_table = jnp.clip(jnp.exp(jax.random.uniform(splits[6], (NMAT,), jnp.float32, math.log(0.5), math.log(4.0))), 0.5, 4.0)
    omega_table = jnp.clip(jnp.exp(jax.random.uniform(splits[7], (NMAT,), jnp.float32, math.log(0.2), math.log(1.2))), 0.2, 1.2)
    damping_table = jnp.clip(jnp.exp(jax.random.uniform(splits[8], (NMAT,), jnp.float32, math.log(0.02), math.log(0.6))), 0.02, 0.6)
    surface_flags = place_ends((jax.random.randint(splits[9], (STRETCHES_X, STRETCHES_Y), 0, 4) < 3).astype(jnp.int32), jax.random.fold_in(splits[9], 1), 0, 1)
    return {"e_field": e_field, "h_field": h_field, "polar": polar, "polar_prev": polar_prev, "material": material, "eps_table": eps_table, "delta_table": delta_table, "omega_table": omega_table, "damping_table": damping_table, "surface_flags": surface_flags}


DT = 0.55
WAVELENGTHS = (5.0, 4.0)

def ahead(field, plane, axis):
    rest = lax.slice_in_dim(field, 1, field.shape[axis], axis=axis)
    return jnp.concatenate([rest, plane], axis=axis) - field

def behind(field, plane, axis):
    rest = lax.slice_in_dim(field, 0, field.shape[axis] - 1, axis=axis)
    return field - jnp.concatenate([plane, rest], axis=axis)

def zero_plane(field, axis):
    shape = list(field.shape)
    shape[axis] = 1
    return jnp.zeros(shape, jnp.float32)

def coefficients(eps_table, delta_table, omega_table, damping_table):
    half = damping_table * (DT / 2.0)
    denom = 1.0 + half
    square = omega_table * omega_table * (DT * DT)
    return ((2.0 - square) / denom, (half - 1.0) / denom, delta_table * square / denom, 1.0 / eps_table)

def curl_e(ex, ey, ez, xnext, ynext):
    zplane = zero_plane(ex, 2)
    curl_x = ahead(ez, ynext[1], 1) - ahead(ey, zplane, 2)
    curl_y = ahead(ex, zplane, 2) - ahead(ez, xnext[1], 0)
    curl_z = ahead(ey, xnext[0], 0) - ahead(ex, ynext[0], 1)
    return (curl_x, curl_y, curl_z)

def curl_h(hx, hy, hz, xprev, yprev):
    zplane = zero_plane(hx, 2)
    curl_x = behind(hz, yprev[1], 1) - behind(hy, zplane, 2)
    curl_y = behind(hx, zplane, 2) - behind(hz, xprev[1], 0)
    curl_z = behind(hy, xprev[0], 0) - behind(hx, yprev[0], 1)
    return (curl_x, curl_y, curl_z)

def directions(start, count):
    index = start + jnp.arange(count, dtype=jnp.int32)
    theta = ((index // NPH).astype(jnp.float32) + 0.5) * (math.pi / 2.0 / NTH)
    phi = ((index % NPH).astype(jnp.float32) + 0.5) * (2.0 * math.pi / NPH)
    return (jnp.sin(theta) * jnp.cos(phi), jnp.sin(theta) * jnp.sin(phi))

def reference(e_field, h_field, polar, polar_prev, material, eps_table, delta_table, omega_table, damping_table, surface_flags):
    coef_a, coef_b, coef_c, coef_inv = coefficients(eps_table, delta_table, omega_table, damping_table)
    vox_a = jnp.take(coef_a, material)
    vox_b = jnp.take(coef_b, material)
    vox_c = jnp.take(coef_c, material)
    vox_inv = jnp.take(coef_inv, material)
    flags = jnp.repeat(jnp.repeat(surface_flags, CX, 0), CY, 1).astype(jnp.float32)
    ex, ey, ez = (e_field[0], e_field[1], e_field[2])
    hx, hy, hz = (h_field[0], h_field[1], h_field[2])
    pols = [polar[0], polar[1], polar[2]]
    prevs = [polar_prev[0], polar_prev[1], polar_prev[2]]
    xz = zero_plane(ex, 0)
    yz = zero_plane(ex, 1)
    real_acc = jnp.zeros((2, 4, NX, NY), jnp.float32)
    imag_acc = jnp.zeros((2, 4, NX, NY), jnp.float32)
    for step in range(2):
        curl_x, curl_y, curl_z = curl_e(ex, ey, ez, (xz, xz), (yz, yz))
        hx = hx - DT * curl_x
        hy = hy - DT * curl_y
        hz = hz - DT * curl_z
        fields = [ex, ey, ez]
        newpol = [vox_a * pols[i] + vox_b * prevs[i] + vox_c * fields[i] for i in range(3)]
        curls = curl_h(hx, hy, hz, (xz, xz), (yz, yz))
        fields = [fields[i] + (DT * curls[i] - (newpol[i] - pols[i])) * vox_inv for i in range(3)]
        ex, ey, ez = fields
        prevs = pols
        pols = newpol
        surface = jnp.stack([-hy[:, :, ZS], hx[:, :, ZS], ey[:, :, ZS], -ex[:, :, ZS]]) * flags[None]
        moment = (step + 1) * DT
        real_acc = real_acc + jnp.stack([surface * math.cos(2.0 * math.pi / WAVELENGTHS[f] * moment) for f in range(2)])
        imag_acc = imag_acc - jnp.stack([surface * math.sin(2.0 * math.pi / WAVELENGTHS[f] * moment) for f in range(2)])
    dir_x, dir_y = directions(0, NDIR)
    ypos = jnp.arange(NY).astype(jnp.float32)

    def row(total, item):
        xpos, real_row, imag_row = item
        parts = []
        for f in range(2):
            wave = 2.0 * math.pi / WAVELENGTHS[f]
            phase = wave * (xpos * dir_x[None, :] + ypos[:, None] * dir_y[None, :])
            cosine = jnp.cos(phase)
            sine = jnp.sin(phase)
            hi = lax.Precision.HIGHEST
            real_part = jnp.dot(real_row[f], cosine, precision=hi) - jnp.dot(imag_row[f], sine, precision=hi)
            imag_part = jnp.dot(real_row[f], sine, precision=hi) + jnp.dot(imag_row[f], cosine, precision=hi)
            parts.append(jnp.stack([real_part, imag_part]))
        return (total + jnp.stack(parts), None)
    rows_x = jnp.arange(NX).astype(jnp.float32)
    total, unused = lax.scan(row, jnp.zeros((2, 2, 4, NDIR), jnp.float32), (rows_x, jnp.moveaxis(real_acc, 2, 0), jnp.moveaxis(imag_acc, 2, 0)))
    far_field = total * (1.0 / math.sqrt(NX * NY))
    return (jnp.stack([ex, ey, ez]), jnp.stack([hx, hy, hz]), jnp.stack(pols), far_field)
```

```python
import functools
import math

import jax
import jax.numpy as jnp
import numpy as np
from jax import lax
from jax.experimental import pallas as pl
from jax.experimental.pallas import tpu as pltpu
from jax.sharding import PartitionSpec as P

NTH = 64
NPH = 256
NDIR = 16384
ZS = 384
DT = 0.55
WAVELENGTHS = (5.0, 4.0)
MESH = pl.DeviceIdType.MESH
F32 = jnp.float32
BF16 = jnp.bfloat16
BY = 8


def step_kernel(
    ngx, ngy, nmat,
    e_in, h_in, p_in, q_in, m_in, eps, delta, omega, damping, flags,
    e_out, h_out, p_out, g_out,
    E, H, PA, PB, MAT, ystage, ye, yh, gather, G,
    in_sem, out_sem, xs_sem, xr_sem, ys_sem, yr_sem, g1s, g1r, g2s, g2r,
):
    cx, cy, nz = MAT.shape
    width = G.shape[2]
    gx = lax.axis_index("gx")
    gy = lax.axis_index("gy")

    loads = [
        pltpu.make_async_copy(e_in, E.at[:, pl.ds(0, cx)], in_sem.at[0]),
        pltpu.make_async_copy(h_in, H.at[:, pl.ds(1, cx)], in_sem.at[1]),
        pltpu.make_async_copy(p_in, PA, in_sem.at[2]),
        pltpu.make_async_copy(q_in, PB, in_sem.at[3]),
        pltpu.make_async_copy(m_in, MAT, in_sem.at[4]),
    ]
    for load in loads:
        load.start()

    barrier = pltpu.get_barrier_semaphore()
    for k in range(1, ngx):
        pl.semaphore_signal(barrier, inc=1, device_id=(lax.rem(gx + k, ngx), gy), device_id_type=MESH)
    for k in range(1, ngy):
        pl.semaphore_signal(barrier, inc=1, device_id=(gx, lax.rem(gy + k, ngy)), device_id_type=MESH)

    @pl.when(gx == ngx - 1)
    def _():
        for c in (1, 2):
            E[c, cx] = jnp.zeros((cy, nz), F32)

    @pl.when(gx == 0)
    def _():
        for c in (1, 2):
            H[c, 0] = jnp.zeros((cy, nz), F32)

    @pl.when(gy == ngy - 1)
    def _():
        ye[...] = jnp.zeros(ye.shape, F32)

    @pl.when(gy == 0)
    def _():
        yh[...] = jnp.zeros(yh.shape, F32)

    def copies(rnd, step):
        if rnd % 2 == 0:
            xsrc, xdst, ydst = E.at[1:3, 0], E.at[1:3, cx], ye.at[step]
            tx, ty = gx - 1, gy - 1
            sends_x, sends_y = gx > 0, gy > 0
            takes_x, takes_y = gx < ngx - 1, gy < ngy - 1
        else:
            xsrc, xdst, ydst = H.at[1:3, cx], H.at[1:3, 0], yh.at[step]
            tx, ty = gx + 1, gy + 1
            sends_x, sends_y = gx < ngx - 1, gy < ngy - 1
            takes_x, takes_y = gx > 0, gy > 0
        xcopy = pltpu.make_async_remote_copy(
            src_ref=xsrc, dst_ref=xdst, send_sem=xs_sem.at[rnd], recv_sem=xr_sem.at[rnd],
            device_id=(lax.rem(tx + ngx, ngx), gy), device_id_type=MESH)
        ycopy = pltpu.make_async_remote_copy(
            src_ref=ystage.at[rnd], dst_ref=ydst, send_sem=ys_sem.at[rnd], recv_sem=yr_sem.at[rnd],
            device_id=(gx, lax.rem(ty + ngy, ngy)), device_id_type=MESH)
        return xcopy, ycopy, sends_x, sends_y, takes_x, takes_y

    def send_x(rnd, step):
        xcopy, _, sends_x, _, _, _ = copies(rnd, step)
        pl.when(sends_x)(xcopy.start)

    def send_y(rnd, step):
        _, ycopy, _, sends_y, _, _ = copies(rnd, step)
        for i, c in enumerate((0, 2)):
            for x in range(cx):
                if rnd % 2 == 0:
                    ystage[rnd, i, x : x + 1, :] = E[c, x, 0:1, :]
                else:
                    ystage[rnd, i, x : x + 1, :] = H[c, x + 1, cy - 1 : cy, :]
        pl.when(sends_y)(ycopy.start)

    def take_x(rnd, step):
        xcopy, _, _, _, takes_x, _ = copies(rnd, step)
        pl.when(takes_x)(xcopy.wait_recv)

    def take_y(rnd, step):
        _, ycopy, _, _, _, takes_y = copies(rnd, step)
        pl.when(takes_y)(ycopy.wait_recv)

    def sent_x(rnd, step):
        xcopy, _, sends_x, _, _, _ = copies(rnd, step)
        pl.when(sends_x)(xcopy.wait_send)

    def sent_y(rnd, step):
        _, ycopy, _, sends_y, _, _ = copies(rnd, step)
        pl.when(sends_y)(ycopy.wait_send)

    row_id = lax.broadcasted_iota(jnp.int32, (BY, nz), 0)
    lane_id = lax.broadcasted_iota(jnp.int32, (BY, nz), 1)

    def up_y(v, row):
        return jnp.where(row_id == BY - 1, row, pltpu.roll(v, BY - 1, 0))

    def up_z(v):
        return jnp.where(lane_id == nz - 1, 0.0, pltpu.roll(v, nz - 1, 1))

    def down_y(v, row):
        return jnp.where(row_id == 0, row, pltpu.roll(v, 1, 0))

    def down_z(v):
        return jnp.where(lane_id == 0, 0.0, pltpu.roll(v, 1, 1))

    def h_plane(step, x):
        for y in range(0, cy, BY):
            here = pl.ds(y, BY)
            ex, ey, ez = E[0, x, here, :], E[1, x, here, :], E[2, x, here, :]
            if y + BY < cy:
                rx, rz = E[0, x, y + BY : y + BY + 1, :], E[2, x, y + BY : y + BY + 1, :]
            else:
                rx, rz = ye[step, 0, pl.ds(x, 1), :], ye[step, 1, pl.ds(x, 1), :]
            eyx, ezx = E[1, x + 1, here, :], E[2, x + 1, here, :]
            curl_x = (up_y(ez, rz) - ez) - (up_z(ey) - ey)
            curl_y = (up_z(ex) - ex) - (ezx - ez)
            curl_z = (eyx - ey) - (up_y(ex, rx) - ex)
            H[0, x + 1, here, :] = H[0, x + 1, here, :] - DT * curl_x
            H[1, x + 1, here, :] = H[1, x + 1, here, :] - DT * curl_y
            H[2, x + 1, here, :] = H[2, x + 1, here, :] - DT * curl_z

    coef = []
    for m in range(nmat):
        half = jnp.full((1, nz), damping[m], F32) * (DT / 2.0)
        denom = 1.0 + half
        om = jnp.full((1, nz), omega[m], F32)
        square = om * om * (DT * DT)
        coef.append((
            (2.0 - square) / denom,
            (half - 1.0) / denom,
            jnp.full((1, nz), delta[m], F32) * square / denom,
            1.0 / jnp.full((1, nz), eps[m], F32),
        ))

    def e_plane(step, x):
        now, old = (PA, PB) if step == 0 else (PB, PA)
        for y in range(0, cy, BY):
            here = pl.ds(y, BY)
            mat = MAT[x, here, :]
            vox = [jnp.broadcast_to(coef[nmat - 1][i], (BY, nz)) for i in range(4)]
            for m in range(nmat - 1):
                hit = mat == m
                vox = [jnp.where(hit, coef[m][i], vox[i]) for i in range(4)]
            a, b, c, inv = vox
            hx, hy, hz = H[0, x + 1, here, :], H[1, x + 1, here, :], H[2, x + 1, here, :]
            if y > 0:
                rx, rz = H[0, x + 1, y - 1 : y, :], H[2, x + 1, y - 1 : y, :]
            else:
                rx, rz = yh[step, 0, pl.ds(x, 1), :], yh[step, 1, pl.ds(x, 1), :]
            hyx, hzx = H[1, x, here, :], H[2, x, here, :]
            curls = (
                (hz - down_y(hz, rz)) - (hy - down_z(hy)),
                (hx - down_z(hx)) - (hz - hzx),
                (hy - hyx) - (hx - down_y(hx, rx)),
            )
            for i in range(3):
                e, p = E[i, x, here, :], now[i, x, here, :]
                new = a * p + b * old[i, x, here, :] + c * e
                E[i, x, here, :] = e + (DT * curls[i] - (new - p)) * inv
                old[i, x, here, :] = new

    flag = flags[0, 0].astype(F32)
    surf_lane = lax.broadcasted_iota(jnp.int32, (cy, width), 1)

    def surface(step):
        def body(x, acc):
            base = (gx * cx + x) * 4
            cols = (
                -H[1, x + 1, :, ZS : ZS + 1], H[0, x + 1, :, ZS : ZS + 1],
                E[1, x, :, ZS : ZS + 1], -E[0, x, :, ZS : ZS + 1],
            )
            for j in range(4):
                acc = jnp.where(surf_lane == base + j, cols[j] * flag, acc)
            return acc

        gather[step, gx] = lax.fori_loop(0, cx, body, jnp.zeros((cy, width), F32))

    def first(step, k):
        return pltpu.make_async_remote_copy(
            src_ref=gather.at[step, gx], dst_ref=gather.at[step, gx],
            send_sem=g1s.at[step, k], recv_sem=g1r.at[step, k],
            device_id=(lax.rem(gx + k, ngx), gy), device_id_type=MESH)

    def second(step, k):
        rows = pl.ds(pl.multiple_of(gy * cy, cy), cy)
        return pltpu.make_async_remote_copy(
            src_ref=G.at[step, rows], dst_ref=G.at[step, rows],
            send_sem=g2s.at[step, k], recv_sem=g2r.at[step, k],
            device_id=(gx, lax.rem(gy + k, ngy)), device_id_type=MESH)

    def gather_first(step):
        for k in range(1, ngx):
            first(step, k).start()

    def gather_second(step):
        for k in range(1, ngx):
            first(step, k).wait()
        total = gather[step, 0]
        for i in range(1, ngx):
            total = total + gather[step, i]
        G[step, pl.ds(pl.multiple_of(gy * cy, cy), cy)] = total
        for k in range(1, ngy):
            second(step, k).start()

    def gather_end(step):
        for k in range(1, ngy):
            second(step, k).wait()

    loads[0].wait()
    pl.semaphore_wait(barrier, ngx + ngy - 2)
    send_x(0, 0)
    send_y(0, 0)
    loads[1].wait()

    for step in range(2):
        down, up = 2 * step, 2 * step + 1
        take_y(down, step)

        @pl.loop(0, cx - 1)
        def _(x):
            h_plane(step, x)

        take_x(down, step)
        h_plane(step, cx - 1)
        send_x(up, step)
        send_y(up, step)
        if step == 0:
            for load in loads[2:]:
                load.wait()
        else:
            pltpu.make_async_copy(H.at[:, pl.ds(1, cx)], h_out, out_sem.at[0]).start()
            gather_second(0)
        sent_x(down, step)
        take_y(up, step)

        @pl.loop(1, cx)
        def _(x):
            e_plane(step, x)

        take_x(up, step)
        e_plane(step, 0)
        if step == 0:
            send_x(2, 1)
            send_y(2, 1)
            sent_x(up, step)
        surface(step)
        gather_first(step)

    saves = [
        pltpu.make_async_copy(H.at[:, pl.ds(1, cx)], h_out, out_sem.at[0]),
        pltpu.make_async_copy(E.at[:, pl.ds(0, cx)], e_out, out_sem.at[1]),
        pltpu.make_async_copy(PA, p_out, out_sem.at[2]),
    ]
    saves[1].start()
    saves[2].start()
    gather_end(0)
    gather_second(1)
    gather_end(1)
    last = pltpu.make_async_copy(G, g_out, out_sem.at[3])
    last.start()
    sent_x(3, 1)
    for rnd in range(4):
        sent_y(rnd, rnd // 2)
    for save in saves:
        save.wait()
    last.wait()


def make_seeds():
    theta = (np.arange(NTH, dtype=np.float64)[:, None] + 0.5) * (math.pi / 2.0 / NTH)
    phi = (np.arange(NPH // 4, dtype=np.float64)[None, :] + 0.5) * (2.0 * math.pi / NPH)
    ux = (np.sin(theta) * np.cos(phi)).reshape(-1)
    uy = (np.sin(theta) * np.sin(phi)).reshape(-1)
    rows = []
    for length in WAVELENGTHS:
        wave = 2.0 * math.pi / length
        for angle in (uy, 8.0 * uy, ux, 2.0 * ux):
            rows += [np.cos(wave * angle), np.sin(wave * angle)]
    return np.stack(rows).astype(np.float32)


def make_spread():
    spread = np.zeros((256, 256), np.float32)
    for r in range(256):
        t, p = (r % 128) // 64, r % 64
        spread[r, t * 128 + (p if r < 128 else 127 - p)] = 1.0
    return spread


TILE = 512


def far_kernel(
    nx, ny, g_ref, seeds, spread, e_in, h_in, p_in, far, e_out, h_out, p_out,
    a_wide, a_low, t_cos, t_sin, s_cos, s_sin, packed, sem,
):
    pid = pl.program_id(0)
    width = 4 * nx
    saves = [
        pltpu.make_async_copy(src, dst, sem.at[i])
        for i, (src, dst) in enumerate(((e_in, e_out), (h_in, h_out), (p_in, p_out)))
    ]

    @pl.when(pid == 0)
    def _():
        for save in saves:
            save.start()
        for s in range(2):
            a = g_ref[s].T
            high = a.astype(BF16)
            rows = pl.ds(s * width, width)
            a_wide[rows, 0:ny] = high
            a_wide[rows, ny : 2 * ny] = high
            a_low[rows, :] = (a - high.astype(F32)).astype(BF16)

    scale = 1.0 / math.sqrt(nx * ny)
    part = 256
    sub = lax.broadcasted_iota(jnp.int32, (8, part), 0)
    for f in range(2):
        omega = 2.0 * math.pi / WAVELENGTHS[f]
        kappa = [math.cos(omega * (s + 1) * DT) * scale for s in range(2)]
        sigma = [math.sin(omega * (s + 1) * DT) * scale for s in range(2)]

        def seed(i, lanes):
            row = 8 * f + i
            return jnp.broadcast_to(seeds[row : row + 1, lanes], (8, part))

        def times(a, b):
            return (a[0] * b[0] - a[1] * b[1], a[0] * b[1] + a[1] * b[0])

        one = jnp.ones((8, part), F32)
        zero = jnp.zeros((8, part), F32)

        def chosen(bit, z):
            on = (sub & bit) != 0
            return (jnp.where(on, z[0], one), jnp.where(on, z[1], zero))

        for o in range(0, TILE, part):
            lanes = slice(o, o + part)
            e1 = (seed(0, lanes), seed(1, lanes))
            e8 = (seed(2, lanes), seed(3, lanes))
            e2 = times(e1, e1)
            e4 = times(e2, e2)
            v = times(times(chosen(1, e1), chosen(2, e2)), chosen(4, e4))
            e16 = times(e8, e8)
            w = times(v, e8)

            def fill(k, carry):
                v, w = (carry[0], carry[1]), (carry[2], carry[3])
                at = pl.multiple_of(k * 16, 16)
                for i, table in ((0, t_cos), (1, t_sin)):
                    full = jnp.concatenate([v[i], w[i]], axis=0)
                    high = full.astype(BF16)
                    table[pl.ds(at, 16), lanes] = high
                    table[pl.ds(pl.multiple_of(at + ny, 16), 16), lanes] = (full - high.astype(F32)).astype(BF16)
                return times(v, e16) + times(w, e16)

            lax.fori_loop(0, ny // 16, fill, v + w, unroll=4)

        for table, result in ((t_cos, s_cos), (t_sin, s_sin)):
            result[...] = jnp.dot(a_wide[...], table[...], preferred_element_type=F32) + jnp.dot(
                a_low[...], table[0:ny, :], preferred_element_type=F32)

        for o in range(0, TILE, part):
            lanes = slice(o, o + part)
            w0 = chosen(4, (seed(4, lanes), seed(5, lanes)))
            e2 = (seed(6, lanes), seed(7, lanes))

            def add(k, carry):
                w, sums = (carry[0], carry[1]), carry[2:]
                fresh = []
                for s in range(2):
                    rows = pl.ds(pl.multiple_of(s * width + k * 8, 8), 8)
                    c, d = s_cos[rows, lanes], s_sin[rows, lanes]
                    fresh += [c * w[0], c * w[1], d * w[0], d * w[1]]
                return times(w, e2) + tuple(t + n for t, n in zip(sums, fresh))

            out = lax.fori_loop(0, nx // 2, add, w0 + (zero,) * 8, unroll=4)
            sums = out[2:]
            re = [zero] * 4
            im = [zero] * 4
            for s in range(2):
                cc, cs, sc, ss = sums[4 * s : 4 * s + 4]
                a, b, c, d = cc - ss, cs + sc, cc + ss, sc - cs
                k, g = kappa[s], sigma[s]
                re[0] += a * k + b * g
                im[0] += b * k - a * g
                re[1] += c * k + d * g
                im[1] += d * k - c * g
                re[2] += a * k - b * g
                im[2] -= b * k + a * g
                re[3] += c * k - d * g
                im[3] -= d * k + c * g
            for q in range(4):
                r = re[q] + pltpu.roll(re[q], 4, 0)
                i = im[q] + pltpu.roll(im[q], 4, 0)
                both = jnp.where(sub < 4, r, i)
                for pair in range(part // 128):
                    at = (((o // 128 + pair) * 2 + f) * 2 + q // 2) * 8
                    packed[at : at + 8, (q % 2) * 128 : (q % 2) * 128 + 128] = both[:, pair * 128 : pair * 128 + 128]

    done = jnp.dot(packed[...], spread[...], precision=lax.Precision.HIGHEST, preferred_element_type=F32)
    for pair in range(TILE // 128):
        for f in range(2):
            for h in range(2):
                at = ((pair * 2 + f) * 2 + h) * 8
                for t in range(2):
                    d = (2 * pair + t) * 256 + h * 128
                    far[f, 0, :, d : d + 128] = done[at : at + 4, t * 128 : t * 128 + 128]
                    far[f, 1, :, d : d + 128] = done[at + 4 : at + 8, t * 128 : t * 128 + 128]

    @pl.when(pid == pl.num_programs(0) - 1)
    def _():
        for save in saves:
            save.wait()


def shards(
    e_field, h_field, polar, polar_prev, material,
    eps_table, delta_table, omega_table, damping_table, surface_flags,
):
    _, cx, cy, nz = e_field.shape
    ngx, ngy = lax.axis_size("gx"), lax.axis_size("gy")
    nx, ny = ngx * cx, ngy * cy
    width = 4 * nx
    hbm = pl.BlockSpec(memory_space=pl.ANY)
    smem = pl.BlockSpec(memory_space=pltpu.SMEM)
    field = jax.ShapeDtypeStruct(e_field.shape, F32)
    dma = pltpu.SemaphoreType.DMA
    e, h, p, g = pl.pallas_call(
        functools.partial(step_kernel, ngx, ngy, eps_table.shape[0]),
        out_shape=(field, field, field, jax.ShapeDtypeStruct((2, ny, width), F32)),
        in_specs=[hbm] * 5 + [smem] * 5,
        out_specs=(hbm,) * 4,
        scratch_shapes=[
            pltpu.VMEM((3, cx + 1, cy, nz), F32),
            pltpu.VMEM((3, cx + 1, cy, nz), F32),
            pltpu.VMEM((3, cx, cy, nz), F32),
            pltpu.VMEM((3, cx, cy, nz), F32),
            pltpu.VMEM((cx, cy, nz), jnp.int32),
            pltpu.VMEM((4, 2, cx, nz), F32),
            pltpu.VMEM((2, 2, cx, nz), F32),
            pltpu.VMEM((2, 2, cx, nz), F32),
            pltpu.VMEM((2, ngx, cy, width), F32),
            pltpu.VMEM((2, ny, width), F32),
            dma((5,)), dma((4,)), dma((4,)), dma((4,)), dma((4,)), dma((4,)),
            dma((2, ngx)), dma((2, ngx)), dma((2, ngy)), dma((2, ngy)),
        ],
        compiler_params=pltpu.CompilerParams(
            collective_id=0, has_side_effects=True, vmem_limit_bytes=24 * 1024 * 1024),
    )(e_field, h_field, polar, polar_prev, material,
      eps_table, delta_table, omega_table, damping_table, surface_flags)

    steps = (NDIR // 4) // TILE
    whole = lambda *shape: pl.BlockSpec(shape, lambda i: (0,) * len(shape))
    far, e, h, p = pl.pallas_call(
        functools.partial(far_kernel, nx, ny),
        grid=(steps,),
        out_shape=(jax.ShapeDtypeStruct((2, 2, 4, NDIR), F32), field, field, field),
        in_specs=[
            whole(2, ny, width),
            pl.BlockSpec((16, TILE), lambda i: (0, i)),
            whole(256, 256),
            hbm, hbm, hbm,
        ],
        out_specs=(pl.BlockSpec((2, 2, 4, 4 * TILE), lambda i: (0, 0, 0, i)), hbm, hbm, hbm),
        scratch_shapes=[
            pltpu.VMEM((2 * width, 2 * ny), BF16),
            pltpu.VMEM((2 * width, ny), BF16),
            pltpu.VMEM((2 * ny, TILE), BF16),
            pltpu.VMEM((2 * ny, TILE), BF16),
            pltpu.VMEM((2 * width, TILE), F32),
            pltpu.VMEM((2 * width, TILE), F32),
            pltpu.VMEM((4 * (TILE // 128) * 8, 256), F32),
            dma((3,)),
        ],
        compiler_params=pltpu.CompilerParams(vmem_limit_bytes=32 * 1024 * 1024),
    )(g, jnp.asarray(make_seeds()), jnp.asarray(make_spread()), e, h, p)
    return e, h, p, far


def solution(mesh):
    cells = P(None, "gx", "gy", None)
    placed = (cells, cells, cells, cells, P("gx", "gy", None), P(), P(), P(), P(), P("gx", "gy"))
    return jax.shard_map(
        shards, mesh=mesh, in_specs=placed, out_specs=(cells, cells, cells, P()), check_vma=False,
    )
```

```python
import functools
import math

import jax
import jax.numpy as jnp
import numpy as np
from jax import lax
from jax.experimental import pallas as pl
from jax.experimental.pallas import tpu as pltpu
from jax.sharding import PartitionSpec as P

NTH = 64
NPH = 256
NDIR = 16384
ZS = 384
DT = 0.55
WAVELENGTHS = (5.0, 4.0)
MESH = pl.DeviceIdType.MESH
F32 = jnp.float32
BF16 = jnp.bfloat16
BY = 8


def coefficients(nmat, nz, eps, delta, omega, damping):
    coef = []
    for m in range(nmat):
        half = jnp.full((1, nz), damping[m], F32) * (DT / 2.0)
        denom = 1.0 + half
        om = jnp.full((1, nz), omega[m], F32)
        square = om * om * (DT * DT)
        coef.append((
            (2.0 - square) / denom,
            (half - 1.0) / denom,
            jnp.full((1, nz), delta[m], F32) * square / denom,
            1.0 / jnp.full((1, nz), eps[m], F32),
        ))
    return coef


def step_kernel(
    ngx, ngy, nmat,
    e_in, h_in, p_in, q_in, m_in, eps_in, delta_in, omega_in, damping_in, flags_in,
    e_out, h_out, p_out, g_out,
    E, H, PA, PB, MAT, ystage, ye, yh, gather, G, eps, delta, omega, damping, flags,
    in_sem, out_sem, xs_sem, xr_sem, ys_sem, yr_sem, g1s, g1r, g2s, g2r,
):
    cx, cy, nz = MAT.shape
    width = G.shape[2]
    gx = lax.axis_index("gx")
    gy = lax.axis_index("gy")

    loads = [
        pltpu.make_async_copy(e_in, E.at[:, pl.ds(0, cx)], in_sem.at[0]),
        pltpu.make_async_copy(h_in, H.at[:, pl.ds(1, cx)], in_sem.at[1]),
        pltpu.make_async_copy(p_in, PA, in_sem.at[2]),
        pltpu.make_async_copy(q_in, PB, in_sem.at[3]),
        pltpu.make_async_copy(m_in, MAT, in_sem.at[4]),
        pltpu.make_async_copy(eps_in, eps, in_sem.at[5]),
        pltpu.make_async_copy(delta_in, delta, in_sem.at[6]),
        pltpu.make_async_copy(omega_in, omega, in_sem.at[7]),
        pltpu.make_async_copy(damping_in, damping, in_sem.at[8]),
        pltpu.make_async_copy(flags_in, flags, in_sem.at[9]),
    ]
    for load in loads:
        load.start()

    barrier = pltpu.get_barrier_semaphore()
    for k in range(1, ngx):
        pl.semaphore_signal(barrier, inc=1, device_id=(lax.rem(gx + k, ngx), gy), device_id_type=MESH)
    for k in range(1, ngy):
        pl.semaphore_signal(barrier, inc=1, device_id=(gx, lax.rem(gy + k, ngy)), device_id_type=MESH)

    @pl.when(gx == ngx - 1)
    def _():
        for c in (1, 2):
            E[c, cx] = jnp.zeros((cy, nz), F32)

    @pl.when(gx == 0)
    def _():
        for c in (1, 2):
            H[c, 0] = jnp.zeros((cy, nz), F32)

    @pl.when(gy == ngy - 1)
    def _():
        ye[...] = jnp.zeros(ye.shape, F32)

    @pl.when(gy == 0)
    def _():
        yh[...] = jnp.zeros(yh.shape, F32)

    def copies(rnd, step):
        if rnd % 2 == 0:
            field, at_src, at_dst, ydst = E, 0, cx, ye.at[step]
            tx, ty = gx - 1, gy - 1
            sends_x, sends_y = gx > 0, gy > 0
            takes_x, takes_y = gx < ngx - 1, gy < ngy - 1
        else:
            field, at_src, at_dst, ydst = H, cx, 0, yh.at[step]
            tx, ty = gx + 1, gy + 1
            sends_x, sends_y = gx < ngx - 1, gy < ngy - 1
            takes_x, takes_y = gx > 0, gy > 0
        xcopies = []
        for i in range(2 * (cy // BY)):
            c, y = 1 + i % 2, (i // 2) * BY
            xcopies.append(pltpu.make_async_remote_copy(
                src_ref=field.at[c, at_src, pl.ds(y, BY)], dst_ref=field.at[c, at_dst, pl.ds(y, BY)],
                send_sem=xs_sem.at[rnd, i], recv_sem=xr_sem.at[rnd, i],
                device_id=(lax.rem(tx + ngx, ngx), gy), device_id_type=MESH))
        ycopy = pltpu.make_async_remote_copy(
            src_ref=ystage.at[rnd], dst_ref=ydst, send_sem=ys_sem.at[rnd], recv_sem=yr_sem.at[rnd],
            device_id=(gx, lax.rem(ty + ngy, ngy)), device_id_type=MESH)
        return xcopies, ycopy, sends_x, sends_y, takes_x, takes_y

    def send_x(rnd, step, block):
        xcopies, _, sends_x, _, _, _ = copies(rnd, step)

        @pl.when(sends_x)
        def _():
            for xcopy in xcopies[2 * block : 2 * block + 2]:
                xcopy.start()

    def send_y(rnd, step):
        _, ycopy, _, sends_y, _, _ = copies(rnd, step)
        for i, c in enumerate((0, 2)):
            for x in range(cx):
                if rnd % 2 == 0:
                    ystage[rnd, i, x : x + 1, :] = E[c, x, 0:1, :]
                else:
                    ystage[rnd, i, x : x + 1, :] = H[c, x + 1, cy - 1 : cy, :]
        pl.when(sends_y)(ycopy.start)

    def take_x(rnd, step, block):
        xcopies, _, _, _, takes_x, _ = copies(rnd, step)

        @pl.when(takes_x)
        def _():
            for xcopy in xcopies[2 * block : 2 * block + 2]:
                xcopy.wait_recv()

    def take_y(rnd, step):
        _, ycopy, _, _, _, takes_y = copies(rnd, step)
        pl.when(takes_y)(ycopy.wait_recv)

    def sent_x(rnd, step):
        xcopies, _, sends_x, _, _, _ = copies(rnd, step)

        @pl.when(sends_x)
        def _():
            for xcopy in xcopies:
                xcopy.wait_send()

    def sent_y(rnd, step):
        _, ycopy, _, sends_y, _, _ = copies(rnd, step)
        pl.when(sends_y)(ycopy.wait_send)

    row_id = lax.broadcasted_iota(jnp.int32, (BY, nz), 0)
    lane_id = lax.broadcasted_iota(jnp.int32, (BY, nz), 1)

    def up_y(v, row):
        return jnp.where(row_id == BY - 1, row, pltpu.roll(v, BY - 1, 0))

    def up_z(v):
        return jnp.where(lane_id == nz - 1, 0.0, pltpu.roll(v, nz - 1, 1))

    def down_y(v, row):
        return jnp.where(row_id == 0, row, pltpu.roll(v, 1, 0))

    def down_z(v):
        return jnp.where(lane_id == 0, 0.0, pltpu.roll(v, 1, 1))

    def h_plane(step, x, blocks):
        for y in [BY * block for block in blocks]:
            here = pl.ds(y, BY)
            ex, ey, ez = E[0, x, here, :], E[1, x, here, :], E[2, x, here, :]
            if y + BY < cy:
                rx, rz = E[0, x, y + BY : y + BY + 1, :], E[2, x, y + BY : y + BY + 1, :]
            else:
                rx, rz = ye[step, 0, pl.ds(x, 1), :], ye[step, 1, pl.ds(x, 1), :]
            eyx, ezx = E[1, x + 1, here, :], E[2, x + 1, here, :]
            curl_x = (up_y(ez, rz) - ez) - (up_z(ey) - ey)
            curl_y = (up_z(ex) - ex) - (ezx - ez)
            curl_z = (eyx - ey) - (up_y(ex, rx) - ex)
            H[0, x + 1, here, :] = H[0, x + 1, here, :] - DT * curl_x
            H[1, x + 1, here, :] = H[1, x + 1, here, :] - DT * curl_y
            H[2, x + 1, here, :] = H[2, x + 1, here, :] - DT * curl_z

    def e_plane(step, x, coef, blocks):
        now, old = (PA, PB) if step == 0 else (PB, PA)
        for y in [BY * block for block in blocks]:
            here = pl.ds(y, BY)
            mat = MAT[x, here, :]
            vox = [jnp.broadcast_to(coef[nmat - 1][i], (BY, nz)) for i in range(4)]
            for m in range(nmat - 1):
                hit = mat == m
                vox = [jnp.where(hit, coef[m][i], vox[i]) for i in range(4)]
            a, b, c, inv = vox
            hx, hy, hz = H[0, x + 1, here, :], H[1, x + 1, here, :], H[2, x + 1, here, :]
            if y > 0:
                rx, rz = H[0, x + 1, y - 1 : y, :], H[2, x + 1, y - 1 : y, :]
            else:
                rx, rz = yh[step, 0, pl.ds(x, 1), :], yh[step, 1, pl.ds(x, 1), :]
            hyx, hzx = H[1, x, here, :], H[2, x, here, :]
            curls = (
                (hz - down_y(hz, rz)) - (hy - down_z(hy)),
                (hx - down_z(hx)) - (hz - hzx),
                (hy - hyx) - (hx - down_y(hx, rx)),
            )
            for i in range(3):
                e, p = E[i, x, here, :], now[i, x, here, :]
                new = a * p + b * old[i, x, here, :] + c * e
                E[i, x, here, :] = e + (DT * curls[i] - (new - p)) * inv
                old[i, x, here, :] = new

    surf_lane = lax.broadcasted_iota(jnp.int32, (cy, width), 1)

    def surface(step, flag):
        def body(x, acc):
            base = (gx * cx + x) * 4
            cols = (
                -H[1, x + 1, :, ZS : ZS + 1], H[0, x + 1, :, ZS : ZS + 1],
                E[1, x, :, ZS : ZS + 1], -E[0, x, :, ZS : ZS + 1],
            )
            for j in range(4):
                acc = jnp.where(surf_lane == base + j, cols[j] * flag, acc)
            return acc

        gather[step, gx] = lax.fori_loop(0, cx, body, jnp.zeros((cy, width), F32))

    def first(step, k):
        return pltpu.make_async_remote_copy(
            src_ref=gather.at[step, gx], dst_ref=gather.at[step, gx],
            send_sem=g1s.at[step, k], recv_sem=g1r.at[step, k],
            device_id=(lax.rem(gx + k, ngx), gy), device_id_type=MESH)

    def second(step, k):
        rows = pl.ds(pl.multiple_of(gy * cy, cy), cy)
        return pltpu.make_async_remote_copy(
            src_ref=G.at[step, rows], dst_ref=G.at[step, rows],
            send_sem=g2s.at[step, k], recv_sem=g2r.at[step, k],
            device_id=(gx, lax.rem(gy + k, ngy)), device_id_type=MESH)

    def gather_first(step):
        for k in range(1, ngx):
            first(step, k).start()

    def gather_second(step):
        for k in range(1, ngx):
            first(step, k).wait()
        total = gather[step, 0]
        for i in range(1, ngx):
            total = total + gather[step, i]
        G[step, pl.ds(pl.multiple_of(gy * cy, cy), cy)] = total
        for k in range(1, ngy):
            second(step, k).start()

    def gather_end(step):
        for k in range(1, ngy):
            second(step, k).wait()

    loads[0].wait()
    pl.semaphore_wait(barrier, ngx + ngy - 2)
    blocks = range(cy // BY)
    send_y(0, 0)
    for block in blocks:
        send_x(0, 0, block)
    for load in loads[1:2] + loads[5:]:
        load.wait()

    coef = coefficients(nmat, nz, eps, delta, omega, damping)
    flag = flags[0, 0].astype(F32)

    for step in range(2):
        down, up = 2 * step, 2 * step + 1
        take_y(down, step)

        @pl.loop(0, cx - 1)
        def _(x):
            h_plane(step, x, blocks)

        for block in blocks:
            take_x(down, step, block)
            h_plane(step, cx - 1, [block])
            send_x(up, step, block)
        send_y(up, step)
        if step == 0:
            for load in loads[2:5]:
                load.wait()
        else:
            pltpu.make_async_copy(H.at[:, pl.ds(1, cx)], h_out, out_sem.at[0]).start()
            gather_second(0)
        sent_x(down, step)
        take_y(up, step)

        @pl.loop(1, cx)
        def _(x):
            e_plane(step, x, coef, blocks)

        for block in blocks:
            take_x(up, step, block)
            e_plane(step, 0, coef, [block])
            if step == 0:
                send_x(2, 1, block)
        if step == 0:
            send_y(2, 1)
            sent_x(up, step)
        surface(step, flag)
        gather_first(step)

    saves = [
        pltpu.make_async_copy(H.at[:, pl.ds(1, cx)], h_out, out_sem.at[0]),
        pltpu.make_async_copy(E.at[:, pl.ds(0, cx)], e_out, out_sem.at[1]),
        pltpu.make_async_copy(PA, p_out, out_sem.at[2]),
    ]
    saves[1].start()
    saves[2].start()
    gather_end(0)
    gather_second(1)
    gather_end(1)
    last = pltpu.make_async_copy(G, g_out, out_sem.at[3])
    last.start()
    sent_x(3, 1)
    for rnd in range(4):
        sent_y(rnd, rnd // 2)
    for save in saves:
        save.wait()
    last.wait()


def make_seeds():
    theta = (np.arange(NTH, dtype=np.float64)[:, None] + 0.5) * (math.pi / 2.0 / NTH)
    phi = (np.arange(NPH // 4, dtype=np.float64)[None, :] + 0.5) * (2.0 * math.pi / NPH)
    ux = (np.sin(theta) * np.cos(phi)).reshape(-1)
    uy = (np.sin(theta) * np.sin(phi)).reshape(-1)
    rows = []
    for length in WAVELENGTHS:
        wave = 2.0 * math.pi / length
        for angle in (uy, 8.0 * uy, ux, 2.0 * ux):
            rows += [np.cos(wave * angle), np.sin(wave * angle)]
    return np.stack(rows).astype(np.float32).reshape(16, -1, TILE).swapaxes(0, 1).copy()


def make_spread():
    spread = np.zeros((256, 256), np.float32)
    for r in range(256):
        t, p = (r % 128) // 64, r % 64
        spread[r, t * 128 + (p if r < 128 else 127 - p)] = 1.0
    return spread


TILE = 512


def far_kernel(
    nx, ny, g_ref, seeds, spread, e_in, h_in, p_in, far, e_out, h_out, p_out,
    a_wide, a_low, t_cos, t_sin, s_cos, s_sin, packed, e_pass, h_pass, p_pass, sem,
):
    pid = pl.program_id(0)
    width = 4 * nx
    tile = pl.num_programs(0) * lax.rem(lax.axis_index("gy"), 2) + pid
    fields = enumerate(zip((e_in, h_in, p_in), (e_pass, h_pass, p_pass), (e_out, h_out, p_out)))
    moves = [
        (pltpu.make_async_copy(src, mid, sem.at[0, i]), pltpu.make_async_copy(mid, dst, sem.at[1, i]))
        for i, (src, mid, dst) in fields
    ]

    @pl.when(pid == 0)
    def _():
        for load, _ in moves:
            load.start()
        for s in range(2):
            a = g_ref[s].T
            high = a.astype(BF16)
            rows = pl.ds(s * width, width)
            a_wide[rows, 0:ny] = high
            a_wide[rows, ny : 2 * ny] = high
            a_low[rows, :] = (a - high.astype(F32)).astype(BF16)

    @pl.when(pid == 1)
    def _():
        for load, save in moves:
            load.wait()
            save.start()

    scale = 1.0 / math.sqrt(nx * ny)
    part = 256
    sub = lax.broadcasted_iota(jnp.int32, (8, part), 0)
    for f in range(2):
        omega = 2.0 * math.pi / WAVELENGTHS[f]
        kappa = [math.cos(omega * (s + 1) * DT) * scale for s in range(2)]
        sigma = [math.sin(omega * (s + 1) * DT) * scale for s in range(2)]

        def seed(i, lanes):
            row = 8 * f + i
            return jnp.broadcast_to(seeds[tile, row : row + 1, lanes], (8, part))

        def times(a, b):
            return (a[0] * b[0] - a[1] * b[1], a[0] * b[1] + a[1] * b[0])

        one = jnp.ones((8, part), F32)
        zero = jnp.zeros((8, part), F32)

        def chosen(bit, z):
            on = (sub & bit) != 0
            return (jnp.where(on, z[0], one), jnp.where(on, z[1], zero))

        for o in range(0, TILE, part):
            lanes = slice(o, o + part)
            e1 = (seed(0, lanes), seed(1, lanes))
            e8 = (seed(2, lanes), seed(3, lanes))
            e2 = times(e1, e1)
            e4 = times(e2, e2)
            v = times(times(chosen(1, e1), chosen(2, e2)), chosen(4, e4))
            e16 = times(e8, e8)
            w = times(v, e8)

            def fill(k, carry):
                v, w = (carry[0], carry[1]), (carry[2], carry[3])
                at = pl.multiple_of(k * 16, 16)
                for i, table in ((0, t_cos), (1, t_sin)):
                    full = jnp.concatenate([v[i], w[i]], axis=0)
                    high = full.astype(BF16)
                    table[pl.ds(at, 16), lanes] = high
                    table[pl.ds(pl.multiple_of(at + ny, 16), 16), lanes] = (full - high.astype(F32)).astype(BF16)
                return times(v, e16) + times(w, e16)

            lax.fori_loop(0, ny // 16, fill, v + w, unroll=4)

        for table, result in ((t_cos, s_cos), (t_sin, s_sin)):
            result[...] = jnp.dot(a_wide[...], table[...], preferred_element_type=F32) + jnp.dot(
                a_low[...], table[0:ny, :], preferred_element_type=F32)

        for o in range(0, TILE, part):
            lanes = slice(o, o + part)
            w0 = chosen(4, (seed(4, lanes), seed(5, lanes)))
            e2 = (seed(6, lanes), seed(7, lanes))

            def add(k, carry):
                w, sums = (carry[0], carry[1]), carry[2:]
                fresh = []
                for s in range(2):
                    rows = pl.ds(pl.multiple_of(s * width + k * 8, 8), 8)
                    c, d = s_cos[rows, lanes], s_sin[rows, lanes]
                    fresh += [c * w[0], c * w[1], d * w[0], d * w[1]]
                return times(w, e2) + tuple(t + n for t, n in zip(sums, fresh))

            out = lax.fori_loop(0, nx // 2, add, w0 + (zero,) * 8, unroll=4)
            sums = out[2:]
            re = [zero] * 4
            im = [zero] * 4
            for s in range(2):
                cc, cs, sc, ss = sums[4 * s : 4 * s + 4]
                a, b, c, d = cc - ss, cs + sc, cc + ss, sc - cs
                k, g = kappa[s], sigma[s]
                re[0] += a * k + b * g
                im[0] += b * k - a * g
                re[1] += c * k + d * g
                im[1] += d * k - c * g
                re[2] += a * k - b * g
                im[2] -= b * k + a * g
                re[3] += c * k - d * g
                im[3] -= d * k + c * g
            for q in range(4):
                r = re[q] + pltpu.roll(re[q], 4, 0)
                i = im[q] + pltpu.roll(im[q], 4, 0)
                both = jnp.where(sub < 4, r, i)
                for pair in range(part // 128):
                    at = (((o // 128 + pair) * 2 + f) * 2 + q // 2) * 8
                    packed[at : at + 8, (q % 2) * 128 : (q % 2) * 128 + 128] = both[:, pair * 128 : pair * 128 + 128]

    done = jnp.dot(packed[...], spread[...], precision=lax.Precision.HIGHEST, preferred_element_type=F32)
    for pair in range(TILE // 128):
        for f in range(2):
            for h in range(2):
                at = ((pair * 2 + f) * 2 + h) * 8
                for t in range(2):
                    d = (2 * pair + t) * 256 + h * 128
                    far[f, 0, :, d : d + 128] = done[at : at + 4, t * 128 : t * 128 + 128]
                    far[f, 1, :, d : d + 128] = done[at + 4 : at + 8, t * 128 : t * 128 + 128]

    @pl.when(pid == pl.num_programs(0) - 1)
    def _():
        for _, save in moves:
            save.wait()


def share_kernel(half, far, slots, sem):
    gx, gy = lax.axis_index("gx"), lax.axis_index("gy")
    core = lax.rem(gy, 2)
    other = (gx, gy + 1 - 2 * core)
    count = half.shape[3]
    barrier = pltpu.get_barrier_semaphore()
    pl.semaphore_signal(barrier, inc=1, device_id=other, device_id_type=MESH)
    pl.semaphore_wait(barrier, 1)
    sends = []
    for i in range(4):
        f, r = i // 2, i % 2
        send = pltpu.make_async_remote_copy(
            src_ref=half.at[f, r], dst_ref=slots.at[f, r], send_sem=sem.at[0, i], recv_sem=sem.at[1, i],
            device_id=other, device_id_type=MESH)
        send.start()
        sends.append(send)
    mine = pl.ds(pl.multiple_of(core * count, count), count)
    theirs = pl.ds(pl.multiple_of((1 - core) * count, count), count)
    far[:, :, :, mine] = half[...]
    for i, send in enumerate(sends):
        f, r = i // 2, i % 2
        send.wait()
        far[f, r, :, theirs] = slots[f, r]


def shards(
    e_field, h_field, polar, polar_prev, material,
    eps_table, delta_table, omega_table, damping_table, surface_flags,
):
    _, cx, cy, nz = e_field.shape
    ngx, ngy = lax.axis_size("gx"), lax.axis_size("gy")
    nx, ny = ngx * cx, ngy * cy
    width = 4 * nx
    hbm = pl.BlockSpec(memory_space=pl.ANY)
    field = jax.ShapeDtypeStruct(e_field.shape, F32)
    dma = pltpu.SemaphoreType.DMA
    e, h, p, g = pl.pallas_call(
        functools.partial(step_kernel, ngx, ngy, eps_table.shape[0]),
        out_shape=(field, field, field, jax.ShapeDtypeStruct((2, ny, width), F32)),
        in_specs=[hbm] * 10,
        out_specs=(hbm,) * 4,
        scratch_shapes=[
            pltpu.VMEM((3, cx + 1, cy, nz), F32),
            pltpu.VMEM((3, cx + 1, cy, nz), F32),
            pltpu.VMEM((3, cx, cy, nz), F32),
            pltpu.VMEM((3, cx, cy, nz), F32),
            pltpu.VMEM((cx, cy, nz), jnp.int32),
            pltpu.VMEM((4, 2, cx, nz), F32),
            pltpu.VMEM((2, 2, cx, nz), F32),
            pltpu.VMEM((2, 2, cx, nz), F32),
            pltpu.VMEM((2, ngx, cy, width), F32),
            pltpu.VMEM((2, ny, width), F32),
            *[pltpu.SMEM(table.shape, F32) for table in (eps_table, delta_table, omega_table, damping_table)],
            pltpu.SMEM(surface_flags.shape, jnp.int32),
            dma((10,)), dma((4,)), dma((4, 2 * (cy // BY))), dma((4, 2 * (cy // BY))), dma((4,)), dma((4,)),
            dma((2, ngx)), dma((2, ngx)), dma((2, ngy)), dma((2, ngy)),
        ],
        compiler_params=pltpu.CompilerParams(
            collective_id=0, has_side_effects=True, vmem_limit_bytes=58 * 1024 * 1024),
    )(e_field, h_field, polar, polar_prev, material,
      eps_table, delta_table, omega_table, damping_table, surface_flags)

    steps = (NDIR // 4) // TILE // 2
    whole = lambda *shape: pl.BlockSpec(shape, lambda i: (0,) * len(shape))
    far, e, h, p = pl.pallas_call(
        functools.partial(far_kernel, nx, ny),
        grid=(steps,),
        out_shape=(jax.ShapeDtypeStruct((2, 2, 4, NDIR // 2), F32), field, field, field),
        in_specs=[
            whole(2, ny, width),
            whole(2 * steps, 16, TILE),
            whole(256, 256),
            hbm, hbm, hbm,
        ],
        out_specs=(pl.BlockSpec((2, 2, 4, 4 * TILE), lambda i: (0, 0, 0, i)), hbm, hbm, hbm),
        scratch_shapes=[
            pltpu.VMEM((2 * width, 2 * ny), BF16),
            pltpu.VMEM((2 * width, ny), BF16),
            pltpu.VMEM((2 * ny, TILE), BF16),
            pltpu.VMEM((2 * ny, TILE), BF16),
            pltpu.VMEM((2 * width, TILE), F32),
            pltpu.VMEM((2 * width, TILE), F32),
            pltpu.VMEM((4 * (TILE // 128) * 8, 256), F32),
            *[pltpu.VMEM(e_field.shape, F32)] * 3,
            dma((2, 3)),
        ],
        compiler_params=pltpu.CompilerParams(vmem_limit_bytes=56 * 1024 * 1024),
    )(g, jnp.asarray(make_seeds()), jnp.asarray(make_spread()), e, h, p)
    far = pl.pallas_call(
        share_kernel,
        out_shape=jax.ShapeDtypeStruct((2, 2, 4, NDIR), F32),
        in_specs=[pl.BlockSpec(memory_space=pltpu.VMEM)],
        out_specs=pl.BlockSpec(memory_space=pltpu.VMEM),
        scratch_shapes=[pltpu.VMEM((2, 2, 4, NDIR // 2), F32), dma((2, 4))],
        compiler_params=pltpu.CompilerParams(
            collective_id=1, has_side_effects=True, vmem_limit_bytes=56 * 1024 * 1024),
    )(far)
    return e, h, p, far


def solution(mesh):
    cells = P(None, "gx", "gy", None)
    placed = (cells, cells, cells, cells, P("gx", "gy", None), P(), P(), P(), P(), P("gx", "gy"))
    return jax.shard_map(
        shards, mesh=mesh, in_specs=placed, out_specs=(cells, cells, cells, P()), check_vma=False,
    )
```

```python
import functools
import math

import jax
import jax.numpy as jnp
import numpy as np
from jax import lax
from jax.experimental import pallas as pl
from jax.experimental.pallas import tpu as pltpu
from jax.sharding import PartitionSpec as P

NTH = 64
NPH = 256
NDIR = 16384
ZS = 384
DT = 0.55
WAVELENGTHS = (5.0, 4.0)
MESH = pl.DeviceIdType.MESH
F32 = jnp.float32
BF16 = jnp.bfloat16
BY = 8


def coefficients(nmat, nz, eps, delta, omega, damping):
    coef = []
    for m in range(nmat):
        half = jnp.full((1, nz), damping[m], F32) * (DT / 2.0)
        denom = 1.0 + half
        om = jnp.full((1, nz), omega[m], F32)
        square = om * om * (DT * DT)
        coef.append((
            (2.0 - square) / denom,
            (half - 1.0) / denom,
            jnp.full((1, nz), delta[m], F32) * square / denom,
            1.0 / jnp.full((1, nz), eps[m], F32),
        ))
    return coef


def step_kernel(
    ngx, ngy, nmat,
    e_in, h_in, p_in, q_in, m_in, eps_in, delta_in, omega_in, damping_in, flags_in,
    e_out, h_out, p_out, g_out,
    E, H, PA, PB, MAT, ystage, ye, yh, gather, G, eps, delta, omega, damping, flags,
    in_sem, out_sem, xs_sem, xr_sem, ys_sem, yr_sem, g1s, g1r, g2s, g2r,
):
    cx, cy, nz = MAT.shape
    width = G.shape[2]
    gx = lax.axis_index("gx")
    gy = lax.axis_index("gy")

    loads = [
        pltpu.make_async_copy(e_in, E.at[:, pl.ds(0, cx)], in_sem.at[0]),
        pltpu.make_async_copy(h_in, H.at[:, pl.ds(1, cx)], in_sem.at[1]),
        pltpu.make_async_copy(p_in, PA, in_sem.at[2]),
        pltpu.make_async_copy(q_in, PB, in_sem.at[3]),
        pltpu.make_async_copy(m_in, MAT, in_sem.at[4]),
        pltpu.make_async_copy(eps_in, eps, in_sem.at[5]),
        pltpu.make_async_copy(delta_in, delta, in_sem.at[6]),
        pltpu.make_async_copy(omega_in, omega, in_sem.at[7]),
        pltpu.make_async_copy(damping_in, damping, in_sem.at[8]),
        pltpu.make_async_copy(flags_in, flags, in_sem.at[9]),
    ]
    for load in loads:
        load.start()

    barrier = pltpu.get_barrier_semaphore()
    for k in range(1, ngx):
        pl.semaphore_signal(barrier, inc=1, device_id=(lax.rem(gx + k, ngx), gy), device_id_type=MESH)
    for k in range(1, ngy):
        pl.semaphore_signal(barrier, inc=1, device_id=(gx, lax.rem(gy + k, ngy)), device_id_type=MESH)

    @pl.when(gx == ngx - 1)
    def _():
        for c in (1, 2):
            E[c, cx] = jnp.zeros((cy, nz), F32)

    @pl.when(gx == 0)
    def _():
        for c in (1, 2):
            H[c, 0] = jnp.zeros((cy, nz), F32)

    @pl.when(gy == ngy - 1)
    def _():
        ye[...] = jnp.zeros(ye.shape, F32)

    @pl.when(gy == 0)
    def _():
        yh[...] = jnp.zeros(yh.shape, F32)

    def copies(rnd, step):
        if rnd % 2 == 0:
            field, at_src, at_dst, ydst = E, 0, cx, ye.at[step]
            tx, ty = gx - 1, gy - 1
            sends_x, sends_y = gx > 0, gy > 0
            takes_x, takes_y = gx < ngx - 1, gy < ngy - 1
        else:
            field, at_src, at_dst, ydst = H, cx, 0, yh.at[step]
            tx, ty = gx + 1, gy + 1
            sends_x, sends_y = gx < ngx - 1, gy < ngy - 1
            takes_x, takes_y = gx > 0, gy > 0
        xcopies = []
        for i in range(2 * (cy // BY)):
            c, y = 1 + i % 2, (i // 2) * BY
            xcopies.append(pltpu.make_async_remote_copy(
                src_ref=field.at[c, at_src, pl.ds(y, BY)], dst_ref=field.at[c, at_dst, pl.ds(y, BY)],
                send_sem=xs_sem.at[rnd, i], recv_sem=xr_sem.at[rnd, i],
                device_id=(lax.rem(tx + ngx, ngx), gy), device_id_type=MESH))
        ycopy = pltpu.make_async_remote_copy(
            src_ref=ystage.at[rnd], dst_ref=ydst, send_sem=ys_sem.at[rnd], recv_sem=yr_sem.at[rnd],
            device_id=(gx, lax.rem(ty + ngy, ngy)), device_id_type=MESH)
        return xcopies, ycopy, sends_x, sends_y, takes_x, takes_y

    def send_x(rnd, step, block):
        xcopies, _, sends_x, _, _, _ = copies(rnd, step)

        @pl.when(sends_x)
        def _():
            for xcopy in xcopies[2 * block : 2 * block + 2]:
                xcopy.start()

    def send_y(rnd, step):
        _, ycopy, _, sends_y, _, _ = copies(rnd, step)
        for i, c in enumerate((0, 2)):
            for x in range(cx):
                if rnd % 2 == 0:
                    ystage[rnd, i, x : x + 1, :] = E[c, x, 0:1, :]
                else:
                    ystage[rnd, i, x : x + 1, :] = H[c, x + 1, cy - 1 : cy, :]
        pl.when(sends_y)(ycopy.start)

    def take_x(rnd, step, block):
        xcopies, _, _, _, takes_x, _ = copies(rnd, step)

        @pl.when(takes_x)
        def _():
            for xcopy in xcopies[2 * block : 2 * block + 2]:
                xcopy.wait_recv()

    def take_y(rnd, step):
        _, ycopy, _, _, _, takes_y = copies(rnd, step)
        pl.when(takes_y)(ycopy.wait_recv)

    def sent_x(rnd, step):
        xcopies, _, sends_x, _, _, _ = copies(rnd, step)

        @pl.when(sends_x)
        def _():
            for xcopy in xcopies:
                xcopy.wait_send()

    def sent_y(rnd, step):
        _, ycopy, _, sends_y, _, _ = copies(rnd, step)
        pl.when(sends_y)(ycopy.wait_send)

    row_id = lax.broadcasted_iota(jnp.int32, (BY, nz), 0)
    lane_id = lax.broadcasted_iota(jnp.int32, (BY, nz), 1)

    def up_y(v, row):
        return jnp.where(row_id == BY - 1, row, pltpu.roll(v, BY - 1, 0))

    def up_z(v):
        return jnp.where(lane_id == nz - 1, 0.0, pltpu.roll(v, nz - 1, 1))

    def down_y(v, row):
        return jnp.where(row_id == 0, row, pltpu.roll(v, 1, 0))

    def down_z(v):
        return jnp.where(lane_id == 0, 0.0, pltpu.roll(v, 1, 1))

    def h_plane(step, x, blocks):
        for y in [BY * block for block in blocks]:
            here = pl.ds(y, BY)
            ex, ey, ez = E[0, x, here, :], E[1, x, here, :], E[2, x, here, :]
            if y + BY < cy:
                rx, rz = E[0, x, y + BY : y + BY + 1, :], E[2, x, y + BY : y + BY + 1, :]
            else:
                rx, rz = ye[step, 0, pl.ds(x, 1), :], ye[step, 1, pl.ds(x, 1), :]
            eyx, ezx = E[1, x + 1, here, :], E[2, x + 1, here, :]
            curl_x = (up_y(ez, rz) - ez) - (up_z(ey) - ey)
            curl_y = (up_z(ex) - ex) - (ezx - ez)
            curl_z = (eyx - ey) - (up_y(ex, rx) - ex)
            H[0, x + 1, here, :] = H[0, x + 1, here, :] - DT * curl_x
            H[1, x + 1, here, :] = H[1, x + 1, here, :] - DT * curl_y
            H[2, x + 1, here, :] = H[2, x + 1, here, :] - DT * curl_z

    def e_plane(step, x, coef, blocks):
        now, old = (PA, PB) if step == 0 else (PB, PA)
        for y in [BY * block for block in blocks]:
            here = pl.ds(y, BY)
            mat = MAT[x, here, :]
            vox = [jnp.broadcast_to(coef[nmat - 1][i], (BY, nz)) for i in range(4)]
            for m in range(nmat - 1):
                hit = mat == m
                vox = [jnp.where(hit, coef[m][i], vox[i]) for i in range(4)]
            a, b, c, inv = vox
            hx, hy, hz = H[0, x + 1, here, :], H[1, x + 1, here, :], H[2, x + 1, here, :]
            if y > 0:
                rx, rz = H[0, x + 1, y - 1 : y, :], H[2, x + 1, y - 1 : y, :]
            else:
                rx, rz = yh[step, 0, pl.ds(x, 1), :], yh[step, 1, pl.ds(x, 1), :]
            hyx, hzx = H[1, x, here, :], H[2, x, here, :]
            curls = (
                (hz - down_y(hz, rz)) - (hy - down_z(hy)),
                (hx - down_z(hx)) - (hz - hzx),
                (hy - hyx) - (hx - down_y(hx, rx)),
            )
            for i in range(3):
                e, p = E[i, x, here, :], now[i, x, here, :]
                new = a * p + b * old[i, x, here, :] + c * e
                E[i, x, here, :] = e + (DT * curls[i] - (new - p)) * inv
                old[i, x, here, :] = new

    surf_lane = lax.broadcasted_iota(jnp.int32, (cy, width), 1)

    def surface(step, flag):
        def body(x, acc):
            base = (gx * cx + x) * 4
            cols = (
                -H[1, x + 1, :, ZS : ZS + 1], H[0, x + 1, :, ZS : ZS + 1],
                E[1, x, :, ZS : ZS + 1], -E[0, x, :, ZS : ZS + 1],
            )
            for j in range(4):
                acc = jnp.where(surf_lane == base + j, cols[j] * flag, acc)
            return acc

        gather[step, gx] = lax.fori_loop(0, cx, body, jnp.zeros((cy, width), F32))

    def first(step, k):
        return pltpu.make_async_remote_copy(
            src_ref=gather.at[step, gx], dst_ref=gather.at[step, gx],
            send_sem=g1s.at[step, k], recv_sem=g1r.at[step, k],
            device_id=(lax.rem(gx + k, ngx), gy), device_id_type=MESH)

    def second(step, k):
        rows = pl.ds(pl.multiple_of(gy * cy, cy), cy)
        return pltpu.make_async_remote_copy(
            src_ref=G.at[step, rows], dst_ref=G.at[step, rows],
            send_sem=g2s.at[step, k], recv_sem=g2r.at[step, k],
            device_id=(gx, lax.rem(gy + k, ngy)), device_id_type=MESH)

    def gather_first(step):
        for k in range(1, ngx):
            first(step, k).start()

    def gather_second(step):
        for k in range(1, ngx):
            first(step, k).wait()
        total = gather[step, 0]
        for i in range(1, ngx):
            total = total + gather[step, i]
        G[step, pl.ds(pl.multiple_of(gy * cy, cy), cy)] = total
        for k in range(1, ngy):
            second(step, k).start()

    def gather_end(step):
        for k in range(1, ngy):
            second(step, k).wait()

    loads[0].wait()
    pl.semaphore_wait(barrier, ngx + ngy - 2)
    blocks = range(cy // BY)
    send_y(0, 0)
    for block in blocks:
        send_x(0, 0, block)
    for load in loads[1:2] + loads[5:]:
        load.wait()

    coef = coefficients(nmat, nz, eps, delta, omega, damping)
    flag = flags[0, 0].astype(F32)

    for step in range(2):
        down, up = 2 * step, 2 * step + 1
        take_y(down, step)

        @pl.loop(0, cx - 1)
        def _(x):
            h_plane(step, x, blocks)

        for block in blocks:
            take_x(down, step, block)
            h_plane(step, cx - 1, [block])
            send_x(up, step, block)
        send_y(up, step)
        if step == 0:
            for load in loads[2:5]:
                load.wait()
        else:
            pltpu.make_async_copy(H.at[:, pl.ds(1, cx)], h_out, out_sem.at[0]).start()
            gather_second(0)
        sent_x(down, step)
        take_y(up, step)

        @pl.loop(1, cx)
        def _(x):
            e_plane(step, x, coef, blocks)

        for block in blocks:
            take_x(up, step, block)
            e_plane(step, 0, coef, [block])
            if step == 0:
                send_x(2, 1, block)
        if step == 0:
            send_y(2, 1)
            sent_x(up, step)
        surface(step, flag)
        gather_first(step)

    saves = [
        pltpu.make_async_copy(H.at[:, pl.ds(1, cx)], h_out, out_sem.at[0]),
        pltpu.make_async_copy(E.at[:, pl.ds(0, cx)], e_out, out_sem.at[1]),
        pltpu.make_async_copy(PA, p_out, out_sem.at[2]),
    ]
    saves[1].start()
    saves[2].start()
    gather_end(0)
    gather_second(1)
    gather_end(1)
    last = pltpu.make_async_copy(G, g_out, out_sem.at[3])
    last.start()
    sent_x(3, 1)
    for rnd in range(4):
        sent_y(rnd, rnd // 2)
    for save in saves:
        save.wait()
    last.wait()


def make_seeds():
    theta = (np.arange(NTH, dtype=np.float64)[:, None] + 0.5) * (math.pi / 2.0 / NTH)
    phi = (np.arange(NPH // 4, dtype=np.float64)[None, :] + 0.5) * (2.0 * math.pi / NPH)
    ux = (np.sin(theta) * np.cos(phi)).reshape(-1)
    uy = (np.sin(theta) * np.sin(phi)).reshape(-1)
    rows = []
    for length in WAVELENGTHS:
        wave = 2.0 * math.pi / length
        for angle in (uy, 8.0 * uy, ux, 2.0 * ux):
            rows += [np.cos(wave * angle), np.sin(wave * angle)]
    return np.stack(rows).astype(np.float32).reshape(16, -1, TILE).swapaxes(0, 1).copy()


def make_spread():
    spread = np.zeros((256, 256), np.float32)
    for r in range(256):
        t, p = (r % 128) // 64, r % 64
        spread[r, t * 128 + (p if r < 128 else 127 - p)] = 1.0
    return spread


TILE = 512


def far_kernel(
    nx, ny, g_ref, seeds, spread, e_in, h_in, p_in, far, e_out, h_out, p_out,
    a_wide, a_low, t_cos, t_sin, s_cos, s_sin, packed, e_pass, h_pass, p_pass, sem,
):
    pid = pl.program_id(0)
    width = 4 * nx
    tile = pl.num_programs(0) * lax.rem(lax.axis_index("gy"), 2) + pid
    fields = enumerate(zip((e_in, h_in, p_in), (e_pass, h_pass, p_pass), (e_out, h_out, p_out)))
    moves = [
        (pltpu.make_async_copy(src, mid, sem.at[0, i]), pltpu.make_async_copy(mid, dst, sem.at[1, i]))
        for i, (src, mid, dst) in fields
    ]

    @pl.when(pid == 0)
    def _():
        for load, _ in moves:
            load.start()
        for s in range(2):
            a = g_ref[s].T
            high = a.astype(BF16)
            rows = pl.ds(s * width, width)
            a_wide[rows, 0:ny] = high
            a_wide[rows, ny : 2 * ny] = high
            a_low[rows, :] = (a - high.astype(F32)).astype(BF16)

    @pl.when(pid == 1)
    def _():
        for load, save in moves:
            load.wait()
            save.start()

    scale = 1.0 / math.sqrt(nx * ny)
    part = 256
    sub = lax.broadcasted_iota(jnp.int32, (8, part), 0)
    for f in range(2):
        omega = 2.0 * math.pi / WAVELENGTHS[f]
        kappa = [math.cos(omega * (s + 1) * DT) * scale for s in range(2)]
        sigma = [math.sin(omega * (s + 1) * DT) * scale for s in range(2)]

        def seed(i, lanes):
            row = 8 * f + i
            return jnp.broadcast_to(seeds[tile, row : row + 1, lanes], (8, part))

        def times(a, b):
            return (a[0] * b[0] - a[1] * b[1], a[0] * b[1] + a[1] * b[0])

        one = jnp.ones((8, part), F32)
        zero = jnp.zeros((8, part), F32)

        def chosen(bit, z):
            on = (sub & bit) != 0
            return (jnp.where(on, z[0], one), jnp.where(on, z[1], zero))

        for o in range(0, TILE, part):
            lanes = slice(o, o + part)
            e1 = (seed(0, lanes), seed(1, lanes))
            e8 = (seed(2, lanes), seed(3, lanes))
            e2 = times(e1, e1)
            e4 = times(e2, e2)
            v = times(times(chosen(1, e1), chosen(2, e2)), chosen(4, e4))
            e16 = times(e8, e8)
            w = times(v, e8)

            def fill(k, carry):
                v, w = (carry[0], carry[1]), (carry[2], carry[3])
                at = pl.multiple_of(k * 16, 16)
                for i, table in ((0, t_cos), (1, t_sin)):
                    full = jnp.concatenate([v[i], w[i]], axis=0)
                    high = full.astype(BF16)
                    table[pl.ds(at, 16), lanes] = high
                    table[pl.ds(pl.multiple_of(at + ny, 16), 16), lanes] = (full - high.astype(F32)).astype(BF16)
                return times(v, e16) + times(w, e16)

            lax.fori_loop(0, ny // 16, fill, v + w, unroll=16)

        for table, result in ((t_cos, s_cos), (t_sin, s_sin)):
            result[...] = jnp.dot(a_wide[...], table[...], preferred_element_type=F32) + jnp.dot(
                a_low[...], table[0:ny, :], preferred_element_type=F32)

        for o in range(0, TILE, part):
            lanes = slice(o, o + part)
            w0 = chosen(4, (seed(4, lanes), seed(5, lanes)))
            e2 = (seed(6, lanes), seed(7, lanes))

            def add(k, carry):
                w, sums = (carry[0], carry[1]), carry[2:]
                fresh = []
                for s in range(2):
                    rows = pl.ds(pl.multiple_of(s * width + k * 8, 8), 8)
                    c, d = s_cos[rows, lanes], s_sin[rows, lanes]
                    fresh += [c * w[0], c * w[1], d * w[0], d * w[1]]
                return times(w, e2) + tuple(t + n for t, n in zip(sums, fresh))

            out = lax.fori_loop(0, nx // 2, add, w0 + (zero,) * 8, unroll=16)
            sums = out[2:]
            re = [zero] * 4
            im = [zero] * 4
            for s in range(2):
                cc, cs, sc, ss = sums[4 * s : 4 * s + 4]
                a, b, c, d = cc - ss, cs + sc, cc + ss, sc - cs
                k, g = kappa[s], sigma[s]
                re[0] += a * k + b * g
                im[0] += b * k - a * g
                re[1] += c * k + d * g
                im[1] += d * k - c * g
                re[2] += a * k - b * g
                im[2] -= b * k + a * g
                re[3] += c * k - d * g
                im[3] -= d * k + c * g
            for q in range(4):
                r = re[q] + pltpu.roll(re[q], 4, 0)
                i = im[q] + pltpu.roll(im[q], 4, 0)
                both = jnp.where(sub < 4, r, i)
                for pair in range(part // 128):
                    at = (((o // 128 + pair) * 2 + f) * 2 + q // 2) * 8
                    packed[at : at + 8, (q % 2) * 128 : (q % 2) * 128 + 128] = both[:, pair * 128 : pair * 128 + 128]

    done = jnp.dot(packed[...], spread[...], precision=lax.Precision.HIGHEST, preferred_element_type=F32)
    for pair in range(TILE // 128):
        for f in range(2):
            for h in range(2):
                at = ((pair * 2 + f) * 2 + h) * 8
                for t in range(2):
                    d = (2 * pair + t) * 256 + h * 128
                    far[f, 0, :, d : d + 128] = done[at : at + 4, t * 128 : t * 128 + 128]
                    far[f, 1, :, d : d + 128] = done[at + 4 : at + 8, t * 128 : t * 128 + 128]

    @pl.when(pid == pl.num_programs(0) - 1)
    def _():
        for _, save in moves:
            save.wait()


def share_kernel(half, far, slots, sem):
    gx, gy = lax.axis_index("gx"), lax.axis_index("gy")
    core = lax.rem(gy, 2)
    other = (gx, gy + 1 - 2 * core)
    count = half.shape[3]
    barrier = pltpu.get_barrier_semaphore()
    pl.semaphore_signal(barrier, inc=1, device_id=other, device_id_type=MESH)
    pl.semaphore_wait(barrier, 1)
    sends = []
    for i in range(4):
        f, r = i // 2, i % 2
        send = pltpu.make_async_remote_copy(
            src_ref=half.at[f, r], dst_ref=slots.at[f, r], send_sem=sem.at[0, i], recv_sem=sem.at[1, i],
            device_id=other, device_id_type=MESH)
        send.start()
        sends.append(send)
    mine = pl.ds(pl.multiple_of(core * count, count), count)
    theirs = pl.ds(pl.multiple_of((1 - core) * count, count), count)
    far[:, :, :, mine] = half[...]
    for i, send in enumerate(sends):
        f, r = i // 2, i % 2
        send.wait()
        far[f, r, :, theirs] = slots[f, r]


def shards(
    e_field, h_field, polar, polar_prev, material,
    eps_table, delta_table, omega_table, damping_table, surface_flags,
):
    _, cx, cy, nz = e_field.shape
    ngx, ngy = lax.axis_size("gx"), lax.axis_size("gy")
    nx, ny = ngx * cx, ngy * cy
    width = 4 * nx
    hbm = pl.BlockSpec(memory_space=pl.ANY)
    field = jax.ShapeDtypeStruct(e_field.shape, F32)
    dma = pltpu.SemaphoreType.DMA
    e, h, p, g = pl.pallas_call(
        functools.partial(step_kernel, ngx, ngy, eps_table.shape[0]),
        out_shape=(field, field, field, jax.ShapeDtypeStruct((2, ny, width), F32)),
        in_specs=[hbm] * 10,
        out_specs=(hbm,) * 4,
        scratch_shapes=[
            pltpu.VMEM((3, cx + 1, cy, nz), F32),
            pltpu.VMEM((3, cx + 1, cy, nz), F32),
            pltpu.VMEM((3, cx, cy, nz), F32),
            pltpu.VMEM((3, cx, cy, nz), F32),
            pltpu.VMEM((cx, cy, nz), jnp.int32),
            pltpu.VMEM((4, 2, cx, nz), F32),
            pltpu.VMEM((2, 2, cx, nz), F32),
            pltpu.VMEM((2, 2, cx, nz), F32),
            pltpu.VMEM((2, ngx, cy, width), F32),
            pltpu.VMEM((2, ny, width), F32),
            *[pltpu.SMEM(table.shape, F32) for table in (eps_table, delta_table, omega_table, damping_table)],
            pltpu.SMEM(surface_flags.shape, jnp.int32),
            dma((10,)), dma((4,)), dma((4, 2 * (cy // BY))), dma((4, 2 * (cy // BY))), dma((4,)), dma((4,)),
            dma((2, ngx)), dma((2, ngx)), dma((2, ngy)), dma((2, ngy)),
        ],
        compiler_params=pltpu.CompilerParams(
            collective_id=0, has_side_effects=True, vmem_limit_bytes=58 * 1024 * 1024),
    )(e_field, h_field, polar, polar_prev, material,
      eps_table, delta_table, omega_table, damping_table, surface_flags)

    steps = (NDIR // 4) // TILE // 2
    whole = lambda *shape: pl.BlockSpec(shape, lambda i: (0,) * len(shape))
    far, e, h, p = pl.pallas_call(
        functools.partial(far_kernel, nx, ny),
        grid=(steps,),
        out_shape=(jax.ShapeDtypeStruct((2, 2, 4, NDIR // 2), F32), field, field, field),
        in_specs=[
            whole(2, ny, width),
            whole(2 * steps, 16, TILE),
            whole(256, 256),
            hbm, hbm, hbm,
        ],
        out_specs=(pl.BlockSpec((2, 2, 4, 4 * TILE), lambda i: (0, 0, 0, i)), hbm, hbm, hbm),
        scratch_shapes=[
            pltpu.VMEM((2 * width, 2 * ny), BF16),
            pltpu.VMEM((2 * width, ny), BF16),
            pltpu.VMEM((2 * ny, TILE), BF16),
            pltpu.VMEM((2 * ny, TILE), BF16),
            pltpu.VMEM((2 * width, TILE), F32),
            pltpu.VMEM((2 * width, TILE), F32),
            pltpu.VMEM((4 * (TILE // 128) * 8, 256), F32),
            *[pltpu.VMEM(e_field.shape, F32)] * 3,
            dma((2, 3)),
        ],
        compiler_params=pltpu.CompilerParams(vmem_limit_bytes=56 * 1024 * 1024),
    )(g, jnp.asarray(make_seeds()), jnp.asarray(make_spread()), e, h, p)
    far = pl.pallas_call(
        share_kernel,
        out_shape=jax.ShapeDtypeStruct((2, 2, 4, NDIR), F32),
        in_specs=[pl.BlockSpec(memory_space=pltpu.VMEM)],
        out_specs=pl.BlockSpec(memory_space=pltpu.VMEM),
        scratch_shapes=[pltpu.VMEM((2, 2, 4, NDIR // 2), F32), dma((2, 4))],
        compiler_params=pltpu.CompilerParams(
            collective_id=1, has_side_effects=True, vmem_limit_bytes=56 * 1024 * 1024),
    )(far)
    return e, h, p, far


def solution(mesh):
    cells = P(None, "gx", "gy", None)
    placed = (cells, cells, cells, cells, P("gx", "gy", None), P(), P(), P(), P(), P("gx", "gy"))
    return jax.shard_map(
        shards, mesh=mesh, in_specs=placed, out_specs=(cells, cells, cells, P()), check_vma=False,
    )
```
